32 devices in a mesh: req: 16 (over z, y, x), blk: 2 (over core).
Axes of the slice: x: 2, y: 2, z: 4, core: 2. Of those that a mesh axis runs over, the one named last changes fastest.
Arguments:
- normed: bfloat16 [8192, 1536], P('req', 'blk'), may hold values from -6 to 6
- router: bfloat16 [1536, 16], P('blk'), may hold values from -0.15625 to 0.15625
- adapter_down: bfloat16 [1536, 256], P('blk'), may hold values from -0.15625 to 0.15625
- adapter_up: bfloat16 [256, 1536], P(None, 'blk'), may hold values from -1.5 to 1.5
- shared_gate_up: bfloat16 [1536, 2, 1024], P(None, None, 'blk'), may hold values from -0.15625 to 0.15625
- shared_down: bfloat16 [1024, 1536], P('blk'), may hold values from -0.1875 to 0.1875
- expert_gate_up: bfloat16 [16, 1536, 1024], P('req', 'blk'), may hold values from -0.15625 to 0.15625
- expert_down: bfloat16 [16, 512, 1536], P('req', None, 'blk'), may hold values from -0.25 to 0.25
- lengths: int32 [16, 4], P('req'), may hold values from 1 to 256, 512 in all within a row
- adapter_ids: int32 [16, 4], P('req'), may hold values from 0 to 15
- routes: int32 [8192, 6], P('req'), may hold values from 0 to 15, all different within a row; in each aligned block of 512 rows (0 to 511, 512 to 1023, ...) at most 208 rows name the same one
Outputs:
- mixed: bfloat16 [8192, 1536], P('req', 'blk')
The draws below stay inside these ranges and needn't reach their ends.
Inputs may be any that keep to these rules, and one draw needn't show every extreme that they name: `lengths`: each row of an index of req lists its 4 prompts in token order; they sum to 512, the longest is 256. `routes`: each row names 6 different experts. Among the 512 rows of one index of req no expert is named more than 208 times, a bound that some block reaches.
All inputs are finite; a program needn't handle non-finite values.
Results may differ from the reference program's by a relative error of at most 0.013.
Values may be sent and summed in bfloat16 or wider, within the bound.
A program may use at most 128 MiB of HBM per device.

```python
import math
import jax
import jax.numpy as jnp
import numpy as np
from jax import lax

D = 1536
FF = 512
SH = 1024
TOPK = 6
ADAPTERS = 16
RANK = 16
REQ_DEV = 4
TOK_DEV = 512
EXPERTS = 16
GROUPS = 16
TOKENS = 8192
PROMPT_MOST = 256
MOST = 208
SLOTS = 3328


def touch_ends(values, stream_key, low, largest):
    shape = values.shape
    spot = [jax.random.randint(jax.random.fold_in(stream_key, axis), (), 0, shape[axis]) for axis in range(len(shape))]
    values = values.at[tuple(spot)].set(low)
    longest = shape.index(max(shape))
    spot[longest] = (spot[longest] + 1) % shape[longest]
    return values.at[tuple(spot)].set(largest)


def level_of(key, dims, shards, smallest, top_value):
    def one(axis_at, parts):
        heights = jax.random.uniform(jax.random.fold_in(jax.random.fold_in(key, 6), axis_at), (parts,), jnp.float32, smallest / len(shards), top_value / len(shards))
        return jnp.repeat(jnp.exp(heights), dims[axis_at] // parts).reshape((-1,) + (1,) * (len(dims) - axis_at - 1))

    factor_of = one(*shards[0])
    for cut in shards[1:]:
        factor_of = factor_of * one(*cut)
    return factor_of


def profile(amount, total, most, lean):
    portions = [(1 << 20) // math.isqrt(grade ** lean) + 1 for grade in range(2, amount + 1)]
    spare, given = total - most - (amount - 1), [1] * (amount - 1)
    while spare > 0:
        movable = [i for i in range(amount - 1) if given[i] < most]
        pool, budget = sum([portions[i] for i in movable]), spare
        for i in movable:
            extra = min(most - given[i], max(1, budget * portions[i] // pool), spare)
            given[i] = given[i] + extra
            spare = spare - extra
    return np.array([most] + given)


def ragged_sizes(own_key, count, total, limit, skew):
    if count == 2:
        one = jax.random.randint(own_key, (), max(1, total - limit), min(limit, total - 1) + 1)
        return jnp.stack([one, total - one])
    sizes = jnp.asarray(profile(count, total, limit, skew), jnp.int32)
    pairs = (count - 1) // 2
    donor, taker = sizes[1:1 + 2 * pairs:2], sizes[2:2 + 2 * pairs:2]
    margin = jnp.minimum(donor - 1, limit - taker)
    passed = jax.random.randint(jax.random.fold_in(own_key, 1), (pairs,), 0, 1 << 20) % (margin + 1)
    sizes = sizes.at[1:1 + 2 * pairs:2].set(donor - passed).at[2:2 + 2 * pairs:2].set(taker + passed)
    return sizes[jax.random.permutation(jax.random.fold_in(own_key, 2), count)]


def assign_block(rng, own, number, rows, number_of, top, most, skew):
    order = jax.random.permutation(rng, number_of)
    heavy_load, usual = load_shares(number_of, rows * top, most, skew, True), load_shares(number_of, rows * top, most, skew, False)
    places = jnp.arange(number_of)

    def named(sizes, rotation):
        used = int((sizes > 0).sum())
        fixed = max(1, used // 4)
        shifted = fixed + (places - fixed + rotation * (used - fixed)) % max(1, number_of - fixed)
        return jnp.zeros((number_of,), jnp.int32).at[order[jnp.where(places < fixed, places, shifted)]].set(jnp.asarray(sizes, jnp.int32))

    sizes = jnp.where(number % 4 == 0, named(heavy_load, number // 4), named(usual, number - number // 4 - 1))
    mixed = jax.random.permutation(jax.random.fold_in(own, 3), number_of)
    donor, taker = mixed[0:number_of // 2 * 2:2], mixed[1:number_of // 2 * 2:2]
    room = jnp.minimum(sizes[donor] - 1, most - sizes[taker]) // 2
    room = jnp.where((donor == order[0]) | (taker == order[0]) | (sizes[taker] == 0), 0, jnp.maximum(room, 0))
    shifted = jax.random.randint(jax.random.fold_in(own, 4), (number_of // 2,), 0, 1 << 20) % (room + 1)
    sizes = sizes.at[donor].add(-shifted).at[taker].add(shifted)
    members = jnp.searchsorted(jnp.cumsum(sizes), jnp.arange(rows * top), side="right").astype(jnp.int32)
    table = members.reshape(top, rows).T
    table = table[jax.random.permutation(jax.random.fold_in(own, 1), rows)]
    rotation = jax.random.randint(jax.random.fold_in(own, 2), (rows, 1), 0, top)
    return jnp.take_along_axis(table, (jnp.arange(top)[None, :] + rotation) % top, axis=1)


def load_shares(amount, total, bound, skew, full):
    portions = [(1 << 20) // math.isqrt(grade ** skew) + 1 for grade in range(1, amount + 1)]
    largest = bound if full else min(bound, max(-(-total // amount), total * portions[0] // sum(portions)))
    least = 1 if total - largest >= amount - 1 else 0
    given, spare = [largest] + [least] * (amount - 1), total - largest - least * (amount - 1)
    while spare > 0:
        movable = [i for i in range(1, amount) if given[i] < largest] or [i for i in range(1, amount) if given[i] < bound]
        mass, left = sum([portions[i] for i in movable]), spare
        for i in movable:
            addition = min(bound - given[i], max(1, left * portions[i] // mass), spare)
            given[i] = given[i] + addition
            spare = spare - addition
    return np.array(given)


def gaussian(rng, dims, width, bound, cuts=(), kind=jnp.bfloat16):
    array = jax.random.normal(rng, dims, jnp.float32) * width
    if len(cuts) > 0:
        array = level_of(rng, dims, cuts, -0.22, 0.18) * array
    return jnp.clip(array, min=-bound, max=bound).astype(kind)


def setup_inputs(seed: int = 0) -> dict:
    arg_keys = jax.random.split(jax.random.key(seed), 12)
    normed = gaussian(arg_keys[0], (TOKENS, D), 1.0, 6.0, ((0, 16), (1, 2)))
    router = gaussian(arg_keys[1], (D, EXPERTS), D ** -0.5, 0.15625, ((0, 2),))
    adapter_down = gaussian(arg_keys[2], (D, ADAPTERS * RANK), D ** -0.5, 0.15625, ((0, 2),))
    adapter_up = gaussian(arg_keys[3], (ADAPTERS * RANK, D), RANK ** -0.5, 1.5, ((1, 2),))
    shared_gate_up = gaussian(arg_keys[4], (D, 2, SH), D ** -0.5, 0.15625, ((2, 2),))
    shared_down = gaussian(arg_keys[5], (SH, D), SH ** -0.5, 0.1875, ((0, 2),))
    expert_gate_up = gaussian(arg_keys[6], (EXPERTS, D, 2 * FF), D ** -0.5, 0.15625, ((0, 16), (1, 2)))
    expert_down = gaussian(arg_keys[7], (EXPERTS, FF, D), FF ** -0.5, 0.25, ((0, 16), (2, 2)))
    lengths = jax.vmap(lambda own: ragged_sizes(own, REQ_DEV, TOK_DEV, PROMPT_MOST, 2))(jax.random.split(arg_keys[8], GROUPS)).reshape((GROUPS, REQ_DEV)).astype(jnp.int32)
    adapter_ids = touch_ends(jax.random.randint(arg_keys[9], (GROUPS, REQ_DEV), 0, ADAPTERS), jax.random.fold_in(arg_keys[9], 1), 0, ADAPTERS - 1).astype(jnp.int32)
    routes_keys = jax.random.split(jax.random.fold_in(arg_keys[10], 1), TOKENS // TOK_DEV)
    routes_turns = jax.random.permutation(jax.random.fold_in(arg_keys[10], 3), TOKENS // TOK_DEV)
    routes = jax.vmap(lambda own, number: assign_block(jax.random.fold_in(arg_keys[10], 2), own, number, TOK_DEV, EXPERTS, TOPK, MOST, 1))(routes_keys, routes_turns).reshape((TOKENS, TOPK))
    return {"normed": normed, "router": router, "adapter_down": adapter_down, "adapter_up": adapter_up, "shared_gate_up": shared_gate_up, "shared_down": shared_down, "expert_gate_up": expert_gate_up, "expert_down": expert_down, "lengths": lengths, "adapter_ids": adapter_ids, "routes": routes}


def reference(normed, router, adapter_down, adapter_up, shared_gate_up, shared_down, expert_gate_up, expert_down, lengths, adapter_ids, routes):
    logits = jnp.dot(normed, router, preferred_element_type=jnp.float32)
    low_all = jnp.dot(normed, adapter_down, preferred_element_type=jnp.float32)
    ends = jnp.cumsum(lengths, axis=1).astype(jnp.int32)
    position = jnp.arange(TOK_DEV, dtype=jnp.int32)
    request = jnp.sum((position[None, :, None] >= ends[:, None, :]).astype(jnp.int32), axis=2).astype(jnp.int32)
    slots_req = jnp.arange(REQ_DEV, dtype=jnp.int32)
    adapter_token = jnp.sum(jnp.where(request[:, :, None] == slots_req[None, None, :], adapter_ids[:, None, :], 0), axis=2).astype(jnp.int32).reshape(-1)
    column_owner = jnp.arange(ADAPTERS * RANK, dtype=jnp.int32) // RANK
    low = jnp.where(column_owner[None, :] == adapter_token[:, None], low_all, 0.0).astype(jnp.bfloat16)
    delta = jnp.dot(low, adapter_up, preferred_element_type=jnp.float32)
    shared_flat = shared_gate_up.reshape(D, 2 * SH)
    shared_pre = jnp.dot(normed, shared_flat, preferred_element_type=jnp.float32)
    shared_hidden = (jax.nn.silu(shared_pre[:, :SH]) * shared_pre[:, SH:]).astype(jnp.bfloat16)
    shared_out = jnp.dot(shared_hidden, shared_down, preferred_element_type=jnp.float32)
    scores = jax.nn.sigmoid(logits)
    chosen = jnp.take_along_axis(scores, routes, axis=1)
    gate_weight = chosen / jnp.sum(chosen, axis=1, keepdims=True)

    def expert_step(total, expert):
        has_route = jnp.any(routes == expert, axis=1)
        row_index = jnp.nonzero(has_route, size=SLOTS, fill_value=0)[0].astype(jnp.int32)
        valid = jnp.arange(SLOTS, dtype=jnp.int32) < jnp.sum(has_route.astype(jnp.int32))
        picked = normed[row_index]
        gate_up = jnp.dot(picked, expert_gate_up[expert], preferred_element_type=jnp.float32)
        hidden = (jax.nn.silu(gate_up[:, :FF]) * gate_up[:, FF:]).astype(jnp.bfloat16)
        result = jnp.dot(hidden, expert_down[expert], preferred_element_type=jnp.float32).astype(jnp.bfloat16)
        result = lax.optimization_barrier(result).astype(jnp.float32)
        weight = jnp.sum(jnp.where(routes[row_index] == expert, gate_weight[row_index], 0.0), axis=1)
        weight = jnp.where(valid, weight, 0.0)
        return total.at[row_index].add(result * weight[:, None]), None

    routed, unused = lax.scan(expert_step, jnp.zeros((TOKENS, D), jnp.float32), jnp.arange(EXPERTS, dtype=jnp.int32))
    return (shared_out + 0.5 * delta + routed).astype(jnp.bfloat16)
```

```python
import jax
import jax.numpy as jnp
from jax import lax
from jax.sharding import PartitionSpec as P

RANK = 16
DEPTH = 4


def body(
    normed,
    router,
    adapter_down,
    adapter_up,
    shared_gate_up,
    shared_down,
    expert_gate_up,
    expert_down,
    lengths,
    adapter_ids,
    routes,
):
    f32, bf16 = jnp.float32, jnp.bfloat16
    tok_rows, feat_local = normed.shape
    feat = 2 * feat_local
    req_count = lax.axis_size("req")
    expert_count = req_count
    plane = req_count // DEPTH
    hidden_width = expert_down.shape[1]
    half = hidden_width // 2
    planes = [[z * plane + p for p in range(plane)] for z in range(DEPTH)]
    columns = [[z * plane + p for z in range(DEPTH)] for p in range(plane)]
    my_z = lax.axis_index("req") // plane

    gu = expert_gate_up[0].reshape(feat_local, 2, 2, half).transpose(2, 0, 1, 3)
    gu = gu.reshape(2 * feat_local, 2 * half)
    gu = lax.all_to_all(gu, "blk", split_axis=0, concat_axis=0, tiled=True)
    down = lax.all_to_all(expert_down[0], "blk", split_axis=0, concat_axis=1, tiled=True)
    gu_all = lax.all_gather(gu, "req", axis_index_groups=planes)
    down_all = lax.all_gather(down, "req", axis_index_groups=planes)

    x_half = lax.all_gather(normed, "req", axis_index_groups=columns, tiled=True)
    x_own = lax.all_gather(normed, "blk", axis=1, tiled=True)
    x_all = lax.all_gather(x_half, "blk", axis=1, tiled=True)

    router_full = lax.all_gather(router, "blk", axis=0, tiled=True)
    logits = jnp.dot(x_own, router_full, preferred_element_type=f32)
    scores = jax.nn.sigmoid(logits)
    experts = jnp.arange(expert_count, dtype=jnp.int32)
    named = jnp.zeros((tok_rows, expert_count), jnp.bool_)
    for k in range(routes.shape[1]):
        named = named | (routes[:, k : k + 1] == experts[None, :])
    chosen = jnp.where(named, scores, 0.0)
    gate = chosen / jnp.sum(chosen, axis=1, keepdims=True)
    gate_all = lax.all_gather(gate, "req", axis_index_groups=columns, tiled=True)
    gate_here = lax.dynamic_slice_in_dim(gate_all, my_z * plane, plane, axis=1)

    low_part = jnp.dot(normed, adapter_down, preferred_element_type=f32)
    low_all = lax.psum(low_part.astype(bf16), "blk").astype(f32)
    ends = jnp.cumsum(lengths[0])
    position = jnp.arange(tok_rows, dtype=jnp.int32)
    request = jnp.sum((position[:, None] >= ends[None, :]).astype(jnp.int32), axis=1)
    slots_req = jnp.arange(lengths.shape[1], dtype=jnp.int32)
    adapter_token = jnp.sum(
        jnp.where(request[:, None] == slots_req[None, :], adapter_ids[0][None, :], 0), axis=1
    )
    column_owner = jnp.arange(low_all.shape[1], dtype=jnp.int32) // RANK
    low = jnp.where(column_owner[None, :] == adapter_token[:, None], low_all, 0.0).astype(bf16)
    delta = jnp.dot(low, adapter_up, preferred_element_type=f32)

    shared_gate = jnp.dot(x_own, shared_gate_up[:, 0, :], preferred_element_type=f32)
    shared_up = jnp.dot(x_own, shared_gate_up[:, 1, :], preferred_element_type=f32)
    shared_hidden = (jax.nn.silu(shared_gate) * shared_up).astype(bf16)
    shared_terms = jnp.dot(shared_hidden, shared_down, preferred_element_type=f32)
    shared_out = lax.psum_scatter(
        shared_terms.astype(bf16), "blk", scatter_dimension=1, tiled=True
    ).astype(f32)

    pieces = []
    for p in range(plane):
        gate_p = jnp.dot(x_all, gu_all[p, :, :half], preferred_element_type=f32)
        up_p = jnp.dot(x_all, gu_all[p, :, half:], preferred_element_type=f32)
        pieces.append((jax.nn.silu(gate_p) * up_p * gate_here[:, p : p + 1]).astype(bf16))
    hidden = jnp.concatenate(pieces, axis=1)
    terms = jnp.dot(hidden, down_all.reshape(plane * half, feat), preferred_element_type=f32)
    terms = lax.psum_scatter(terms.astype(bf16), "blk", scatter_dimension=1, tiled=True)
    routed = lax.psum_scatter(
        terms, "req", scatter_dimension=0, axis_index_groups=columns, tiled=True
    ).astype(f32)
    return (shared_out + 0.5 * delta + routed).astype(bf16)


def solution(mesh):
    return jax.shard_map(
        body,
        mesh=mesh,
        in_specs=(
            P("req", "blk"),
            P("blk", None),
            P("blk", None),
            P(None, "blk"),
            P(None, None, "blk"),
            P("blk", None),
            P("req", "blk", None),
            P("req", None, "blk"),
            P("req", None),
            P("req", None),
            P("req", None),
        ),
        out_specs=P("req", "blk"),
        check_vma=False,
    )
```

```python
import jax
import jax.numpy as jnp
from jax import lax
from jax.experimental import pallas as pl
from jax.experimental.pallas import tpu as pltpu
from jax.sharding import PartitionSpec as P

RANK = 16
DEPTH = 4


def gather_kernel(x, gu, down, x_all, gu_all, down_all, local, tok_send, tok_recv, w_send, w_recv):
    req, c = lax.axis_index("req"), lax.axis_index("blk")
    z, p = req // 4, req % 4
    px = (p // 2) * 2 + 1 - p % 2
    py = (1 - p // 2) * 2 + p % 2
    pd = (1 - p // 2) * 2 + 1 - p % 2
    s = 1 - c
    rows, width = x.shape
    dev = lambda r, b: {"device_id": (r, b), "device_id_type": pl.DeviceIdType.MESH}
    rx, ry = z * 4 + px, z * 4 + py

    barrier = pltpu.get_barrier_semaphore()
    signal = lambda r, b: pl.semaphore_signal(barrier, inc=1, **dev(r, b))
    signal(req, s)
    for b in range(2):
        signal(rx, b)
        signal(ry, b)

    @pl.when(z > 0)
    def _():
        signal(req - 4, c)

    @pl.when(z < 3)
    def _():
        signal(req + 4, c)

    pl.semaphore_wait(barrier, 5 + jnp.where(z > 0, 1, 0) + jnp.where(z < 3, 1, 0))

    def place(zz, b):
        return x_all.at[
            pl.ds(pl.multiple_of(zz * rows, rows), rows), pl.ds(pl.multiple_of(b * width, width), width)
        ]

    def tok(src, zz, k_send, k_recv, r, b):
        return pltpu.make_async_remote_copy(
            src_ref=src, dst_ref=place(zz, c), send_sem=tok_send.at[k_send], recv_sem=tok_recv.at[k_recv], **dev(r, b)
        )

    def weights(src_gu, src_down, owner, part, k_send, rel, r, b):
        return (
            pltpu.make_async_remote_copy(
                src_ref=src_gu, dst_ref=gu_all.at[owner, part], send_sem=w_send.at[0, k_send],
                recv_sem=w_recv.at[0, rel, part], **dev(r, b)
            ),
            pltpu.make_async_remote_copy(
                src_ref=src_down, dst_ref=down_all.at[part, owner], send_sem=w_send.at[1, k_send],
                recv_sem=w_recv.at[1, rel, part], **dev(r, b)
            ),
        )

    up = lambda d: tok(x if d == 0 else place(z - d, c), z - d, d, d, req + 4, c)
    dn = lambda d: tok(x if d == 0 else place(z + d, c), z + d, 3 + d, 3 + d, req - 4, c)
    sib_own = tok(x, z, 6, 6, req, s)
    sib_up = lambda d: tok(place(z - d, c), z - d, 6 + d, 6 + d, req, s)
    sib_dn = lambda d: tok(place(z + d, c), z + d, 9 + d, 9 + d, req, s)

    pl.when(z < 3)(lambda: up(0).start())
    pl.when(z > 0)(lambda: dn(0).start())

    sends = []
    for k, (r, rel) in enumerate(((rx, 1), (ry, 2))):
        for t in range(2):
            sends += list(weights(gu.at[t], down.at[t], p, c, 2 * k + t, rel, r, t))
    for copy in sends:
        copy.start()
    own = weights(gu.at[s], down.at[s], p, c, 4, 0, req, s)
    for copy in own:
        copy.start()
    sib_own.start()
    here = (
        pltpu.make_async_copy(x, place(z, c), local.at[0]),
        pltpu.make_async_copy(gu.at[c], gu_all.at[p, c], local.at[1]),
        pltpu.make_async_copy(down.at[c], down_all.at[c, p], local.at[2]),
    )
    for copy in here:
        copy.start()

    for d in range(1, 4):

        @pl.when(z >= d)
        def _():
            up(d - 1).wait_recv()
            if d < 3:
                pl.when(z < 3)(lambda: up(d).start())
            sib_up(d).start()

        @pl.when(z + d <= 3)
        def _():
            dn(d - 1).wait_recv()
            if d < 3:
                pl.when(z > 0)(lambda: dn(d).start())
            sib_dn(d).start()

    def arrived(owner, part, rel):
        for copy in weights(gu_all.at[owner, part], down_all.at[part, owner], owner, part, 0, rel, req, s):
            copy.wait_recv()

    arrived(px, 0, 1)
    fwd_y = weights(gu_all.at[px, 0], down_all.at[0, px], px, 0, 5, 3, ry, c)
    for copy in fwd_y:
        copy.start()
    arrived(py, 1, 2)
    fwd_x = weights(gu_all.at[py, 1], down_all.at[1, py], py, 1, 6, 3, rx, c)
    for copy in fwd_x:
        copy.start()
    arrived(px, 1, 1)
    arrived(py, 0, 2)
    for copy in weights(gu.at[s], down.at[s], p, s, 4, 0, req, s):
        copy.wait_recv()
    arrived(pd, 0, 3)
    arrived(pd, 1, 3)
    for copy in here:
        copy.wait()
    for copy in sends:
        copy.wait_send()
    for copy in own + fwd_y + fwd_x:
        copy.wait_send()
    sib_own.wait()
    for d in range(1, 4):

        @pl.when(z >= d)
        def _():
            sib_up(d).wait()

        @pl.when(z + d <= 3)
        def _():
            sib_dn(d).wait()

    for d in range(3):

        @pl.when((z >= d) & (z < 3))
        def _():
            up(d).wait_send()

        @pl.when((z + d <= 3) & (z > 0))
        def _():
            dn(d).wait_send()


def gather(x, gu, down):
    rows, width = x.shape
    any_space = pl.BlockSpec(memory_space=pl.ANY)
    return pl.pallas_call(
        gather_kernel,
        out_shape=(
            jax.ShapeDtypeStruct((4 * rows, 2 * width), x.dtype),
            jax.ShapeDtypeStruct((4,) + gu.shape, x.dtype),
            jax.ShapeDtypeStruct((2, 4) + down.shape[1:], x.dtype),
        ),
        in_specs=[any_space] * 3,
        out_specs=(any_space,) * 3,
        scratch_shapes=[
            pltpu.SemaphoreType.DMA((3,)),
            pltpu.SemaphoreType.DMA((13,)),
            pltpu.SemaphoreType.DMA((13,)),
            pltpu.SemaphoreType.DMA((2, 7)),
            pltpu.SemaphoreType.DMA((2, 4, 2)),
        ],
        compiler_params=pltpu.CompilerParams(collective_id=0, has_side_effects=True),
    )(x, gu, down)


def body(
    normed,
    router,
    adapter_down,
    adapter_up,
    shared_gate_up,
    shared_down,
    expert_gate_up,
    expert_down,
    lengths,
    adapter_ids,
    routes,
):
    f32, bf16 = jnp.float32, jnp.bfloat16
    tok_rows, feat_local = normed.shape
    feat = 2 * feat_local
    req_count = lax.axis_size("req")
    expert_count = req_count
    plane = req_count // DEPTH
    hidden_width = expert_down.shape[1]
    half = hidden_width // 2
    planes = [[z * plane + p for p in range(plane)] for z in range(DEPTH)]
    columns = [[z * plane + p for z in range(DEPTH)] for p in range(plane)]
    my_z = lax.axis_index("req") // plane

    gu = expert_gate_up[0].reshape(feat_local, 2, 2, half).transpose(2, 0, 1, 3)
    gu = gu.reshape(2, feat_local, 2 * half)
    down = expert_down[0].reshape(2, half, feat_local)
    routes_all = lax.all_gather(routes, "req", axis_index_groups=columns, tiled=True)
    router_full = lax.all_gather(router, "blk", axis=0, tiled=True)
    if plane == 4:
        x_all, gu_all, down_all = gather(normed, gu, down)
        gu_all = gu_all.reshape(plane, feat, 2 * half)
    else:
        gu = lax.all_to_all(gu, "blk", split_axis=0, concat_axis=0).reshape(feat, 2 * half)
        down = lax.all_to_all(down, "blk", split_axis=0, concat_axis=0)
        gu_all = lax.all_gather(gu, "req", axis_index_groups=planes)
        down_all = lax.all_gather(down, "req", axis=1, axis_index_groups=planes)
        x_half = lax.all_gather(normed, "req", axis_index_groups=columns, tiled=True)
        x_all = lax.all_gather(x_half, "blk", axis=1, tiled=True)
    x_own = lax.dynamic_slice_in_dim(x_all, my_z * tok_rows, tok_rows, axis=0)

    logits = jnp.dot(x_all, router_full, preferred_element_type=f32)
    scores = jax.nn.sigmoid(logits)
    experts = jnp.arange(expert_count, dtype=jnp.int32)
    named = jnp.zeros(scores.shape, jnp.bool_)
    for k in range(routes.shape[1]):
        named = named | (routes_all[:, k : k + 1] == experts[None, :])
    chosen = jnp.where(named, scores, 0.0)
    gate_all = chosen / jnp.sum(chosen, axis=1, keepdims=True)
    gate_here = lax.dynamic_slice_in_dim(gate_all, my_z * plane, plane, axis=1)

    low_part = jnp.dot(normed, adapter_down, preferred_element_type=f32)
    low_all = lax.psum(low_part.astype(bf16), "blk").astype(f32)
    ends = jnp.cumsum(lengths[0])
    position = jnp.arange(tok_rows, dtype=jnp.int32)
    request = jnp.sum((position[:, None] >= ends[None, :]).astype(jnp.int32), axis=1)
    slots_req = jnp.arange(lengths.shape[1], dtype=jnp.int32)
    adapter_token = jnp.sum(
        jnp.where(request[:, None] == slots_req[None, :], adapter_ids[0][None, :], 0), axis=1
    )
    column_owner = jnp.arange(low_all.shape[1], dtype=jnp.int32) // RANK
    low = jnp.where(column_owner[None, :] == adapter_token[:, None], low_all, 0.0).astype(bf16)
    delta = jnp.dot(low, adapter_up, preferred_element_type=f32)

    shared_gate = jnp.dot(x_own, shared_gate_up[:, 0, :], preferred_element_type=f32)
    shared_up = jnp.dot(x_own, shared_gate_up[:, 1, :], preferred_element_type=f32)
    shared_hidden = (jax.nn.silu(shared_gate) * shared_up).astype(bf16)
    shared_terms = jnp.dot(shared_hidden, shared_down, preferred_element_type=f32)
    shared_out = lax.psum_scatter(
        shared_terms.astype(bf16), "blk", scatter_dimension=1, tiled=True
    ).astype(f32)

    pieces = []
    for p in range(plane):
        gate_p = jnp.dot(x_all, gu_all[p, :, :half], preferred_element_type=f32)
        up_p = jnp.dot(x_all, gu_all[p, :, half:], preferred_element_type=f32)
        pieces.append((jax.nn.silu(gate_p) * up_p * gate_here[:, p : p + 1]).astype(bf16))
    hidden = jnp.concatenate(pieces, axis=1)
    terms = jnp.concatenate(
        [
            jnp.dot(hidden, down_all[b].reshape(plane * half, feat_local), preferred_element_type=f32)
            for b in range(2)
        ],
        axis=1,
    )
    terms = lax.psum_scatter(terms.astype(bf16), "blk", scatter_dimension=1, tiled=True)
    routed = lax.psum_scatter(
        terms, "req", scatter_dimension=0, axis_index_groups=columns, tiled=True
    ).astype(f32)
    return (shared_out + 0.5 * delta + routed).astype(bf16)


def solution(mesh):
    return jax.shard_map(
        body,
        mesh=mesh,
        in_specs=(
            P("req", "blk"),
            P("blk", None),
            P("blk", None),
            P(None, "blk"),
            P(None, None, "blk"),
            P("blk", None),
            P("req", "blk", None),
            P("req", None, "blk"),
            P("req", None),
            P("req", None),
            P("req", None),
        ),
        out_specs=P("req", "blk"),
        check_vma=False,
    )
```

```python
import jax
import jax.numpy as jnp
from jax import lax
from jax.experimental import pallas as pl
from jax.experimental.pallas import tpu as pltpu
from jax.sharding import PartitionSpec as P

RANK = 16
DEPTH = 4


def gather_kernel(
    x, gu, down, rt, ro, ad, x_all, gu_all, down_all, rt_all, ro_all, ad_all,
    local, tok_send, tok_recv, w_send, w_recv, s_send, s_recv,
):
    req, c = lax.axis_index("req"), lax.axis_index("blk")
    z, p = req // 4, req % 4
    px = (p // 2) * 2 + 1 - p % 2
    py = (1 - p // 2) * 2 + p % 2
    pd = (1 - p // 2) * 2 + 1 - p % 2
    s = 1 - c
    rows, width = x.shape
    dev = lambda r, b: {"device_id": (r, b), "device_id_type": pl.DeviceIdType.MESH}
    rx, ry = z * 4 + px, z * 4 + py

    barrier = pltpu.get_barrier_semaphore()
    signal = lambda r, b: pl.semaphore_signal(barrier, inc=1, **dev(r, b))
    signal(req, s)
    for b in range(2):
        signal(rx, b)
        signal(ry, b)

    for d in range(1, 4):
        signal(((z + d) % 4) * 4 + p, c)
    pl.semaphore_wait(barrier, 8)
    small = [
        pltpu.make_async_remote_copy(
            src_ref=rt, dst_ref=rt_all.at[z], send_sem=s_send.at[d - 1], recv_sem=s_recv.at[d - 1],
            **dev(((z + d) % 4) * 4 + p, c)
        )
        for d in range(1, 4)
    ] + [
        pltpu.make_async_remote_copy(
            src_ref=src, dst_ref=dst.at[c], send_sem=s_send.at[k], recv_sem=s_recv.at[k], **dev(req, s)
        )
        for k, src, dst in ((3, ro, ro_all), (4, ad, ad_all))
    ]
    for copy in small:
        copy.start()

    def place(zz, b):
        return x_all.at[
            pl.ds(pl.multiple_of(zz * rows, rows), rows), pl.ds(pl.multiple_of(b * width, width), width)
        ]

    def tok(src, zz, k_send, k_recv, r, b):
        return pltpu.make_async_remote_copy(
            src_ref=src, dst_ref=place(zz, c), send_sem=tok_send.at[k_send], recv_sem=tok_recv.at[k_recv], **dev(r, b)
        )

    def weights(src_gu, src_down, owner, part, k_send, rel, r, b):
        return (
            pltpu.make_async_remote_copy(
                src_ref=src_gu, dst_ref=gu_all.at[owner, part], send_sem=w_send.at[0, k_send],
                recv_sem=w_recv.at[0, rel, part], **dev(r, b)
            ),
            pltpu.make_async_remote_copy(
                src_ref=src_down, dst_ref=down_all.at[part, owner], send_sem=w_send.at[1, k_send],
                recv_sem=w_recv.at[1, rel, part], **dev(r, b)
            ),
        )

    up = lambda d: tok(x if d == 0 else place(z - d, c), z - d, d, d, req + 4, c)
    dn = lambda d: tok(x if d == 0 else place(z + d, c), z + d, 3 + d, 3 + d, req - 4, c)
    sib_own = tok(x, z, 6, 6, req, s)
    sib_up = lambda d: tok(place(z - d, c), z - d, 6 + d, 6 + d, req, s)
    sib_dn = lambda d: tok(place(z + d, c), z + d, 9 + d, 9 + d, req, s)

    pl.when(z < 3)(lambda: up(0).start())
    pl.when(z > 0)(lambda: dn(0).start())

    sends = []
    for k, (r, rel) in enumerate(((rx, 1), (ry, 2))):
        for t in range(2):
            sends += list(weights(gu.at[t], down.at[t], p, c, 2 * k + t, rel, r, t))
    for copy in sends:
        copy.start()
    own = weights(gu.at[s], down.at[s], p, c, 4, 0, req, s)
    for copy in own:
        copy.start()
    sib_own.start()
    here = (
        pltpu.make_async_copy(x, place(z, c), local.at[0]),
        pltpu.make_async_copy(gu.at[c], gu_all.at[p, c], local.at[1]),
        pltpu.make_async_copy(down.at[c], down_all.at[c, p], local.at[2]),
        pltpu.make_async_copy(rt, rt_all.at[z], local.at[3]),
        pltpu.make_async_copy(ro, ro_all.at[c], local.at[4]),
        pltpu.make_async_copy(ad, ad_all.at[c], local.at[5]),
    )
    for copy in here:
        copy.start()

    for d in range(1, 4):

        @pl.when(z >= d)
        def _():
            up(d - 1).wait_recv()
            if d < 3:
                pl.when(z < 3)(lambda: up(d).start())
            sib_up(d).start()

        @pl.when(z + d <= 3)
        def _():
            dn(d - 1).wait_recv()
            if d < 3:
                pl.when(z > 0)(lambda: dn(d).start())
            sib_dn(d).start()

    def arrived(owner, part, rel):
        for copy in weights(gu_all.at[owner, part], down_all.at[part, owner], owner, part, 0, rel, req, s):
            copy.wait_recv()

    arrived(px, 0, 1)
    fwd_y = weights(gu_all.at[px, 0], down_all.at[0, px], px, 0, 5, 3, ry, c)
    for copy in fwd_y:
        copy.start()
    arrived(py, 1, 2)
    fwd_x = weights(gu_all.at[py, 1], down_all.at[1, py], py, 1, 6, 3, rx, c)
    for copy in fwd_x:
        copy.start()
    arrived(px, 1, 1)
    arrived(py, 0, 2)
    for copy in weights(gu.at[s], down.at[s], p, s, 4, 0, req, s):
        copy.wait_recv()
    arrived(pd, 0, 3)
    arrived(pd, 1, 3)
    for copy in here + tuple(small):
        copy.wait()
    for copy in sends:
        copy.wait_send()
    for copy in own + fwd_y + fwd_x:
        copy.wait_send()
    sib_own.wait()
    for d in range(1, 4):

        @pl.when(z >= d)
        def _():
            sib_up(d).wait()

        @pl.when(z + d <= 3)
        def _():
            sib_dn(d).wait()

    for d in range(3):

        @pl.when((z >= d) & (z < 3))
        def _():
            up(d).wait_send()

        @pl.when((z + d <= 3) & (z > 0))
        def _():
            dn(d).wait_send()


def gather(x, gu, down, rt, ro, ad):
    rows, width = x.shape
    any_space = pl.BlockSpec(memory_space=pl.ANY)
    return pl.pallas_call(
        gather_kernel,
        out_shape=(
            jax.ShapeDtypeStruct((4 * rows, 2 * width), x.dtype),
            jax.ShapeDtypeStruct((4,) + gu.shape, x.dtype),
            jax.ShapeDtypeStruct((2, 4) + down.shape[1:], x.dtype),
            jax.ShapeDtypeStruct((4,) + rt.shape, rt.dtype),
            jax.ShapeDtypeStruct((2,) + ro.shape, ro.dtype),
            jax.ShapeDtypeStruct((2,) + ad.shape, ad.dtype),
        ),
        in_specs=[any_space] * 6,
        out_specs=(any_space,) * 6,
        scratch_shapes=[
            pltpu.SemaphoreType.DMA((6,)),
            pltpu.SemaphoreType.DMA((13,)),
            pltpu.SemaphoreType.DMA((13,)),
            pltpu.SemaphoreType.DMA((2, 7)),
            pltpu.SemaphoreType.DMA((2, 4, 2)),
            pltpu.SemaphoreType.DMA((5,)),
            pltpu.SemaphoreType.DMA((5,)),
        ],
        compiler_params=pltpu.CompilerParams(collective_id=0, has_side_effects=True),
    )(x, gu, down, rt, ro, ad)


def return_kernel(t, sh, out, sib, below, above, sh_in, sib_send, sib_recv, z_send, up_recv, dn_recv):
    req, c = lax.axis_index("req"), lax.axis_index("blk")
    z, s = req // 4, 1 - c
    rows = sh.shape[1]
    step = rows // 4
    dev = lambda r, b: {"device_id": (r, b), "device_id_type": pl.DeviceIdType.MESH}
    barrier = pltpu.get_barrier_semaphore()
    pl.semaphore_signal(barrier, inc=1, **dev(req, s))

    @pl.when(z > 0)
    def _():
        pl.semaphore_signal(barrier, inc=1, **dev(req - 4, c))

    @pl.when(z < 3)
    def _():
        pl.semaphore_signal(barrier, inc=1, **dev(req + 4, c))

    pl.semaphore_wait(barrier, 1 + jnp.where(z > 0, 1, 0) + jnp.where(z < 3, 1, 0))

    def pair(src, dst, k):
        return pltpu.make_async_remote_copy(
            src_ref=src, dst_ref=dst, send_sem=sib_send.at[k], recv_sem=sib_recv.at[k], **dev(req, s)
        )

    def chain(k, dst, recv, r):
        return pltpu.make_async_remote_copy(
            src_ref=sib.at[k], dst_ref=dst.at[k], send_sem=z_send.at[k], recv_sem=recv.at[k], **dev(r, c)
        )

    order = (3, 0, 2, 1)
    across = {k: pair(t.at[s, k], sib.at[k], k) for k in order}
    across[4] = pair(sh.at[s], sh_in, 4)
    for copy in across.values():
        copy.start()

    def add_into(k, other):
        def one(i, carry):
            at = pl.ds(pl.multiple_of(i * step, step), step)
            sib[k, at, :] = (sib[k, at, :].astype(jnp.float32) + other(at).astype(jnp.float32)).astype(sib.dtype)
            return carry

        lax.fori_loop(0, 4, one, 0)

    def add_pair(k, other):
        def one(i, carry):
            at = pl.ds(pl.multiple_of(i * step, step), step)
            total = sib[k, at, :].astype(jnp.float32) + t[c, k, at, :].astype(jnp.float32)
            sib[k, at, :] = (total + other[k, at, :].astype(jnp.float32)).astype(sib.dtype)
            return carry

        lax.fori_loop(0, 4, one, 0)

    for k in order:
        across[k].wait_recv()

        if k > 0:

            @pl.when((z < k) & (z > 0))
            def _():
                chain(k, below, up_recv, req + 4).wait_recv()
                add_pair(k, below)

            @pl.when((z < k) & (z == 0))
            def _():
                add_into(k, lambda at: t[c, k, at, :])

            @pl.when(z < k)
            def _():
                chain(k, below, up_recv, req + 4).start()

        if k < 3:

            @pl.when((z > k) & (z < 3))
            def _():
                chain(k, above, dn_recv, req - 4).wait_recv()
                add_pair(k, above)

            @pl.when((z > k) & (z == 3))
            def _():
                add_into(k, lambda at: t[c, k, at, :])

            @pl.when(z > k)
            def _():
                chain(k, above, dn_recv, req - 4).start()

    across[4].wait_recv()
    f32 = jnp.float32

    def first(i, carry):
        at = pl.ds(pl.multiple_of(i * step, step), step)
        total = sib[z, at, :].astype(f32) + t[c, z, at, :].astype(f32)
        out[at, :] = total + sh[c, at, :].astype(f32) + sh_in[at, :].astype(f32)
        return carry

    lax.fori_loop(0, 4, first, 0)

    def more(buffer):
        def one(i, carry):
            at = pl.ds(pl.multiple_of(i * step, step), step)
            out[at, :] += buffer[z, at, :].astype(f32)
            return carry

        lax.fori_loop(0, 4, one, 0)

    @pl.when(z > 0)
    def _():
        chain(z, below, up_recv, req + 4).wait_recv()
        more(below)

    @pl.when(z < 3)
    def _():
        chain(z, above, dn_recv, req - 4).wait_recv()
        more(above)

    for copy in across.values():
        copy.wait_send()
    for k in order:

        @pl.when(z != k)
        def _():
            chain(k, below, up_recv, req + 4).wait_send()


def give_back(t, sh):
    block = t.shape[1:]
    vmem = pl.BlockSpec(memory_space=pltpu.VMEM)
    return pl.pallas_call(
        return_kernel,
        out_shape=jax.ShapeDtypeStruct(block[1:], jnp.float32),
        in_specs=[vmem, vmem],
        out_specs=vmem,
        scratch_shapes=[
            pltpu.VMEM(block, t.dtype),
            pltpu.VMEM(block, t.dtype),
            pltpu.VMEM(block, t.dtype),
            pltpu.VMEM(block[1:], t.dtype),
            pltpu.SemaphoreType.DMA((5,)),
            pltpu.SemaphoreType.DMA((5,)),
            pltpu.SemaphoreType.DMA((4,)),
            pltpu.SemaphoreType.DMA((4,)),
            pltpu.SemaphoreType.DMA((4,)),
        ],
        compiler_params=pltpu.CompilerParams(
            collective_id=1, has_side_effects=True, vmem_limit_bytes=48 * 1024 * 1024
        ),
    )(t, sh)


def body(
    normed,
    router,
    adapter_down,
    adapter_up,
    shared_gate_up,
    shared_down,
    expert_gate_up,
    expert_down,
    lengths,
    adapter_ids,
    routes,
):
    f32, bf16 = jnp.float32, jnp.bfloat16
    tok_rows, feat_local = normed.shape
    feat = 2 * feat_local
    req_count = lax.axis_size("req")
    expert_count = req_count
    plane = req_count // DEPTH
    hidden_width = expert_down.shape[1]
    half = hidden_width // 2
    planes = [[z * plane + p for p in range(plane)] for z in range(DEPTH)]
    columns = [[z * plane + p for z in range(DEPTH)] for p in range(plane)]
    my_z = lax.axis_index("req") // plane

    gu = expert_gate_up[0].reshape(feat_local, 2, 2, half).transpose(2, 0, 1, 3)
    gu = gu.reshape(2, feat_local, 2 * half)
    down = expert_down[0].reshape(2, half, feat_local)
    if plane == 4:
        x_all, gu_all, down_all, routes_all, router_full, adapter_full = gather(
            normed, gu, down, routes.T, router, adapter_down
        )
        routes_all = routes_all.transpose(0, 2, 1).reshape(DEPTH * tok_rows, routes.shape[1])
        router_full = router_full.reshape(feat, expert_count)
        adapter_full = adapter_full.reshape(feat, adapter_down.shape[1])
        gu_all = gu_all.reshape(plane, feat, 2 * half)
    else:
        routes_all = lax.all_gather(routes, "req", axis_index_groups=columns, tiled=True)
        router_full = lax.all_gather(router, "blk", axis=0, tiled=True)
        adapter_full = lax.all_gather(adapter_down, "blk", axis=0, tiled=True)
        gu = lax.all_to_all(gu, "blk", split_axis=0, concat_axis=0).reshape(feat, 2 * half)
        down = lax.all_to_all(down, "blk", split_axis=0, concat_axis=0)
        gu_all = lax.all_gather(gu, "req", axis_index_groups=planes)
        down_all = lax.all_gather(down, "req", axis=1, axis_index_groups=planes)
        x_half = lax.all_gather(normed, "req", axis_index_groups=columns, tiled=True)
        x_all = lax.all_gather(x_half, "blk", axis=1, tiled=True)
    x_own = lax.dynamic_slice_in_dim(x_all, my_z * tok_rows, tok_rows, axis=0)

    logits = jnp.dot(x_all, router_full, preferred_element_type=f32)
    scores = jax.nn.sigmoid(logits)
    experts = jnp.arange(expert_count, dtype=jnp.int32)
    named = jnp.zeros(scores.shape, jnp.bool_)
    for k in range(routes.shape[1]):
        named = named | (routes_all[:, k : k + 1] == experts[None, :])
    chosen = jnp.where(named, scores, 0.0)
    gate_all = chosen / jnp.sum(chosen, axis=1, keepdims=True)
    gate_here = lax.dynamic_slice_in_dim(gate_all, my_z * plane, plane, axis=1)

    low_all = jnp.dot(x_own, adapter_full, preferred_element_type=f32)
    ends = jnp.cumsum(lengths[0])
    position = jnp.arange(tok_rows, dtype=jnp.int32)
    request = jnp.sum((position[:, None] >= ends[None, :]).astype(jnp.int32), axis=1)
    slots_req = jnp.arange(lengths.shape[1], dtype=jnp.int32)
    adapter_token = jnp.sum(
        jnp.where(request[:, None] == slots_req[None, :], adapter_ids[0][None, :], 0), axis=1
    )
    column_owner = jnp.arange(low_all.shape[1], dtype=jnp.int32) // RANK
    low = jnp.where(column_owner[None, :] == adapter_token[:, None], low_all, 0.0).astype(bf16)
    delta = jnp.dot(low, adapter_up, preferred_element_type=f32)

    shared_gate = jnp.dot(x_own, shared_gate_up[:, 0, :], preferred_element_type=f32)
    shared_up = jnp.dot(x_own, shared_gate_up[:, 1, :], preferred_element_type=f32)
    shared_hidden = (jax.nn.silu(shared_gate) * shared_up).astype(bf16)
    shared_terms = jnp.dot(shared_hidden, shared_down, preferred_element_type=f32)
    pieces = []
    for p in range(plane):
        gate_p = jnp.dot(x_all, gu_all[p, :, :half], preferred_element_type=f32)
        up_p = jnp.dot(x_all, gu_all[p, :, half:], preferred_element_type=f32)
        pieces.append((jax.nn.silu(gate_p) * up_p * gate_here[:, p : p + 1]).astype(bf16))
    hidden = jnp.concatenate(pieces, axis=1)
    terms = [
        jnp.dot(hidden, down_all[b].reshape(plane * half, feat_local), preferred_element_type=f32).astype(bf16)
        for b in range(2)
    ]
    shared_terms = shared_terms.astype(bf16)
    if plane == 4:
        parts = jnp.stack([x.reshape(DEPTH, tok_rows, feat_local) for x in terms])
        shared_parts = jnp.stack([shared_terms[:, :feat_local], shared_terms[:, feat_local:]])
        summed = give_back(parts, shared_parts)
    else:
        shared_out = lax.psum_scatter(shared_terms, "blk", scatter_dimension=1, tiled=True)
        terms = lax.psum_scatter(jnp.concatenate(terms, axis=1), "blk", scatter_dimension=1, tiled=True)
        summed = shared_out.astype(f32) + lax.psum_scatter(
            terms, "req", scatter_dimension=0, axis_index_groups=columns, tiled=True
        ).astype(f32)
    return (summed + 0.5 * delta).astype(bf16)


def solution(mesh):
    return jax.shard_map(
        body,
        mesh=mesh,
        in_specs=(
            P("req", "blk"),
            P("blk", None),
            P("blk", None),
            P(None, "blk"),
            P(None, None, "blk"),
            P("blk", None),
            P("req", "blk", None),
            P("req", None, "blk"),
            P("req", None),
            P("req", None),
            P("req", None),
        ),
        out_specs=P("req", "blk"),
        check_vma=False,
    )
```

```python
import jax
import jax.numpy as jnp
from jax import lax
from jax.experimental import pallas as pl
from jax.experimental.pallas import tpu as pltpu
from jax.sharding import PartitionSpec as P

RANK = 16
DEPTH = 4


def gather_kernel(
    x, gu, down, rt, ro, ad, x_all, gu_all, down_all, rt_all, ro_all, ad_all,
    local, tok_send, tok_recv, w_send, w_recv, s_send, s_recv,
):
    req, c = lax.axis_index("req"), lax.axis_index("blk")
    z, p = req // 4, req % 4
    px = (p // 2) * 2 + 1 - p % 2
    py = (1 - p // 2) * 2 + p % 2
    pd = (1 - p // 2) * 2 + 1 - p % 2
    s = 1 - c
    rows, width = x.shape
    dev = lambda r, b: {"device_id": (r, b), "device_id_type": pl.DeviceIdType.MESH}
    rx, ry = z * 4 + px, z * 4 + py

    barrier = pltpu.get_barrier_semaphore()
    signal = lambda r, b: pl.semaphore_signal(barrier, inc=1, **dev(r, b))
    signal(req, s)
    for b in range(2):
        signal(rx, b)
        signal(ry, b)

    for d in range(1, 4):
        signal(((z + d) % 4) * 4 + p, c)
    pl.semaphore_wait(barrier, 8)
    small = [
        pltpu.make_async_remote_copy(
            src_ref=rt, dst_ref=rt_all.at[z], send_sem=s_send.at[d - 1], recv_sem=s_recv.at[d - 1],
            **dev(((z + d) % 4) * 4 + p, c)
        )
        for d in range(1, 4)
    ] + [
        pltpu.make_async_remote_copy(
            src_ref=src, dst_ref=dst.at[c], send_sem=s_send.at[k], recv_sem=s_recv.at[k], **dev(req, s)
        )
        for k, src, dst in ((3, ro, ro_all), (4, ad, ad_all))
    ]
    for copy in small:
        copy.start()

    def place(zz, b):
        return x_all.at[
            pl.ds(pl.multiple_of(zz * rows, rows), rows), pl.ds(pl.multiple_of(b * width, width), width)
        ]

    def tok(src, zz, k_send, k_recv, r, b):
        return pltpu.make_async_remote_copy(
            src_ref=src, dst_ref=place(zz, c), send_sem=tok_send.at[k_send], recv_sem=tok_recv.at[k_recv], **dev(r, b)
        )

    def weights(src_gu, src_down, owner, part, k_send, rel, r, b):
        return (
            pltpu.make_async_remote_copy(
                src_ref=src_gu, dst_ref=gu_all.at[owner, part], send_sem=w_send.at[0, k_send],
                recv_sem=w_recv.at[0, rel, part], **dev(r, b)
            ),
            pltpu.make_async_remote_copy(
                src_ref=src_down, dst_ref=down_all.at[part, owner], send_sem=w_send.at[1, k_send],
                recv_sem=w_recv.at[1, rel, part], **dev(r, b)
            ),
        )

    up = lambda d: tok(x if d == 0 else place(z - d, c), z - d, d, d, req + 4, c)
    dn = lambda d: tok(x if d == 0 else place(z + d, c), z + d, 3 + d, 3 + d, req - 4, c)
    sib_own = tok(x, z, 6, 6, req, s)
    sib_up = lambda d: tok(place(z - d, c), z - d, 6 + d, 6 + d, req, s)
    sib_dn = lambda d: tok(place(z + d, c), z + d, 9 + d, 9 + d, req, s)

    pl.when(z < 3)(lambda: up(0).start())
    pl.when(z > 0)(lambda: dn(0).start())

    sends = []
    for k, (r, rel) in enumerate(((rx, 1), (ry, 2))):
        for t in range(2):
            sends += list(weights(gu.at[t], down.at[t], p, c, 2 * k + t, rel, r, t))
    for copy in sends:
        copy.start()
    own = weights(gu.at[s], down.at[s], p, c, 4, 0, req, s)
    for copy in own:
        copy.start()
    sib_own.start()
    here = (
        pltpu.make_async_copy(x, place(z, c), local.at[0]),
        pltpu.make_async_copy(gu.at[c], gu_all.at[p, c], local.at[1]),
        pltpu.make_async_copy(down.at[c], down_all.at[c, p], local.at[2]),
        pltpu.make_async_copy(rt, rt_all.at[z], local.at[3]),
        pltpu.make_async_copy(ro, ro_all.at[c], local.at[4]),
        pltpu.make_async_copy(ad, ad_all.at[c], local.at[5]),
    )
    for copy in here:
        copy.start()

    for d in range(1, 4):

        @pl.when(z >= d)
        def _():
            up(d - 1).wait_recv()
            if d < 3:
                pl.when(z < 3)(lambda: up(d).start())
            sib_up(d).start()

        @pl.when(z + d <= 3)
        def _():
            dn(d - 1).wait_recv()
            if d < 3:
                pl.when(z > 0)(lambda: dn(d).start())
            sib_dn(d).start()

    def arrived(owner, part, rel):
        for copy in weights(gu_all.at[owner, part], down_all.at[part, owner], owner, part, 0, rel, req, s):
            copy.wait_recv()

    arrived(px, 0, 1)
    fwd_y = weights(gu_all.at[px, 0], down_all.at[0, px], px, 0, 5, 3, ry, c)
    for copy in fwd_y:
        copy.start()
    arrived(py, 1, 2)
    fwd_x = weights(gu_all.at[py, 1], down_all.at[1, py], py, 1, 6, 3, rx, c)
    for copy in fwd_x:
        copy.start()
    arrived(px, 1, 1)
    arrived(py, 0, 2)
    for copy in weights(gu.at[s], down.at[s], p, s, 4, 0, req, s):
        copy.wait_recv()
    arrived(pd, 0, 3)
    arrived(pd, 1, 3)
    for copy in here + tuple(small):
        copy.wait()
    for copy in sends:
        copy.wait_send()
    for copy in own + fwd_y + fwd_x:
        copy.wait_send()
    sib_own.wait()
    for d in range(1, 4):

        @pl.when(z >= d)
        def _():
            sib_up(d).wait()

        @pl.when(z + d <= 3)
        def _():
            sib_dn(d).wait()

    for d in range(3):

        @pl.when((z >= d) & (z < 3))
        def _():
            up(d).wait_send()

        @pl.when((z + d <= 3) & (z > 0))
        def _():
            dn(d).wait_send()


def gather(x, gu, down, rt, ro, ad):
    rows, width = x.shape
    any_space = pl.BlockSpec(memory_space=pl.ANY)
    return pl.pallas_call(
        gather_kernel,
        out_shape=(
            jax.ShapeDtypeStruct((4 * rows, 2 * width), x.dtype),
            jax.ShapeDtypeStruct((4,) + gu.shape, x.dtype),
            jax.ShapeDtypeStruct((2, 4) + down.shape[1:], x.dtype),
            jax.ShapeDtypeStruct((4,) + rt.shape, rt.dtype),
            jax.ShapeDtypeStruct((2,) + ro.shape, ro.dtype),
            jax.ShapeDtypeStruct((2,) + ad.shape, ad.dtype),
        ),
        in_specs=[any_space] * 6,
        out_specs=(any_space,) * 6,
        scratch_shapes=[
            pltpu.SemaphoreType.DMA((6,)),
            pltpu.SemaphoreType.DMA((13,)),
            pltpu.SemaphoreType.DMA((13,)),
            pltpu.SemaphoreType.DMA((2, 7)),
            pltpu.SemaphoreType.DMA((2, 4, 2)),
            pltpu.SemaphoreType.DMA((5,)),
            pltpu.SemaphoreType.DMA((5,)),
        ],
        compiler_params=pltpu.CompilerParams(collective_id=0, has_side_effects=True),
    )(x, gu, down, rt, ro, ad)


def return_kernel(t, sh, out, sib, below, above, sh_in, sib_send, sib_recv, z_send, up_recv, dn_recv):
    req, c = lax.axis_index("req"), lax.axis_index("blk")
    z, s = req // 4, 1 - c
    rows = sh.shape[1]
    step = rows // 4
    dev = lambda r, b: {"device_id": (r, b), "device_id_type": pl.DeviceIdType.MESH}
    barrier = pltpu.get_barrier_semaphore()
    pl.semaphore_signal(barrier, inc=1, **dev(req, s))

    @pl.when(z > 0)
    def _():
        pl.semaphore_signal(barrier, inc=1, **dev(req - 4, c))

    @pl.when(z < 3)
    def _():
        pl.semaphore_signal(barrier, inc=1, **dev(req + 4, c))

    pl.semaphore_wait(barrier, 1 + jnp.where(z > 0, 1, 0) + jnp.where(z < 3, 1, 0))

    def pair(src, dst, k):
        return pltpu.make_async_remote_copy(
            src_ref=src, dst_ref=dst, send_sem=sib_send.at[k], recv_sem=sib_recv.at[k], **dev(req, s)
        )

    def chain(k, dst, recv, r):
        return pltpu.make_async_remote_copy(
            src_ref=sib.at[k], dst_ref=dst.at[k], send_sem=z_send.at[k], recv_sem=recv.at[k], **dev(r, c)
        )

    order = [k + (z // 2) * (3 - 2 * k) for k in (3, 0, 2, 1)]
    across = [pair(t.at[s, k], sib.at[k], k) for k in order] + [pair(sh.at[s], sh_in, 4)]
    for copy in across:
        copy.start()

    def add_into(k, other):
        def one(i, carry):
            at = pl.ds(pl.multiple_of(i * step, step), step)
            sib[k, at, :] = (sib[k, at, :].astype(jnp.float32) + other(at).astype(jnp.float32)).astype(sib.dtype)
            return carry

        lax.fori_loop(0, 4, one, 0)

    def add_pair(k, other):
        def one(i, carry):
            at = pl.ds(pl.multiple_of(i * step, step), step)
            total = sib[k, at, :].astype(jnp.float32) + t[c, k, at, :].astype(jnp.float32)
            sib[k, at, :] = (total + other[k, at, :].astype(jnp.float32)).astype(sib.dtype)
            return carry

        lax.fori_loop(0, 4, one, 0)

    for i, k in enumerate(order):
        across[i].wait_recv()

        if True:

            @pl.when((z < k) & (z > 0))
            def _():
                chain(k, below, up_recv, req + 4).wait_recv()
                add_pair(k, below)

            @pl.when((z < k) & (z == 0))
            def _():
                add_into(k, lambda at: t[c, k, at, :])

            @pl.when(z < k)
            def _():
                chain(k, below, up_recv, req + 4).start()

        if True:

            @pl.when((z > k) & (z < 3))
            def _():
                chain(k, above, dn_recv, req - 4).wait_recv()
                add_pair(k, above)

            @pl.when((z > k) & (z == 3))
            def _():
                add_into(k, lambda at: t[c, k, at, :])

            @pl.when(z > k)
            def _():
                chain(k, above, dn_recv, req - 4).start()

    across[4].wait_recv()
    f32 = jnp.float32

    def first(i, carry):
        at = pl.ds(pl.multiple_of(i * step, step), step)
        total = sib[z, at, :].astype(f32) + t[c, z, at, :].astype(f32)
        out[at, :] = total + sh[c, at, :].astype(f32) + sh_in[at, :].astype(f32)
        return carry

    lax.fori_loop(0, 4, first, 0)

    def more(buffer):
        def one(i, carry):
            at = pl.ds(pl.multiple_of(i * step, step), step)
            out[at, :] += buffer[z, at, :].astype(f32)
            return carry

        lax.fori_loop(0, 4, one, 0)

    @pl.when(z > 0)
    def _():
        chain(z, below, up_recv, req + 4).wait_recv()
        more(below)

    @pl.when(z < 3)
    def _():
        chain(z, above, dn_recv, req - 4).wait_recv()
        more(above)

    for copy in across:
        copy.wait_send()
    for k in order:

        @pl.when(z != k)
        def _():
            chain(k, below, up_recv, req + 4).wait_send()


def give_back(t, sh):
    block = t.shape[1:]
    vmem = pl.BlockSpec(memory_space=pltpu.VMEM)
    return pl.pallas_call(
        return_kernel,
        out_shape=jax.ShapeDtypeStruct(block[1:], jnp.float32),
        in_specs=[vmem, vmem],
        out_specs=vmem,
        scratch_shapes=[
            pltpu.VMEM(block, t.dtype),
            pltpu.VMEM(block, t.dtype),
            pltpu.VMEM(block, t.dtype),
            pltpu.VMEM(block[1:], t.dtype),
            pltpu.SemaphoreType.DMA((5,)),
            pltpu.SemaphoreType.DMA((5,)),
            pltpu.SemaphoreType.DMA((4,)),
            pltpu.SemaphoreType.DMA((4,)),
            pltpu.SemaphoreType.DMA((4,)),
        ],
        compiler_params=pltpu.CompilerParams(
            collective_id=1, has_side_effects=True, vmem_limit_bytes=48 * 1024 * 1024
        ),
    )(t, sh)


def body(
    normed,
    router,
    adapter_down,
    adapter_up,
    shared_gate_up,
    shared_down,
    expert_gate_up,
    expert_down,
    lengths,
    adapter_ids,
    routes,
):
    f32, bf16 = jnp.float32, jnp.bfloat16
    tok_rows, feat_local = normed.shape
    feat = 2 * feat_local
    req_count = lax.axis_size("req")
    expert_count = req_count
    plane = req_count // DEPTH
    hidden_width = expert_down.shape[1]
    half = hidden_width // 2
    planes = [[z * plane + p for p in range(plane)] for z in range(DEPTH)]
    columns = [[z * plane + p for z in range(DEPTH)] for p in range(plane)]
    my_z = lax.axis_index("req") // plane

    gu = expert_gate_up[0].reshape(feat_local, 2, 2, half).transpose(2, 0, 1, 3)
    gu = gu.reshape(2, feat_local, 2 * half)
    down = expert_down[0].reshape(2, half, feat_local)
    if plane == 4:
        x_all, gu_all, down_all, routes_all, router_full, adapter_full = gather(
            normed, gu, down, routes.T, router, adapter_down
        )
        routes_all = routes_all.transpose(0, 2, 1).reshape(DEPTH * tok_rows, routes.shape[1])
        router_full = router_full.reshape(feat, expert_count)
        adapter_full = adapter_full.reshape(feat, adapter_down.shape[1])
        gu_all = gu_all.reshape(plane, feat, 2 * half)
    else:
        routes_all = lax.all_gather(routes, "req", axis_index_groups=columns, tiled=True)
        router_full = lax.all_gather(router, "blk", axis=0, tiled=True)
        adapter_full = lax.all_gather(adapter_down, "blk", axis=0, tiled=True)
        gu = lax.all_to_all(gu, "blk", split_axis=0, concat_axis=0).reshape(feat, 2 * half)
        down = lax.all_to_all(down, "blk", split_axis=0, concat_axis=0)
        gu_all = lax.all_gather(gu, "req", axis_index_groups=planes)
        down_all = lax.all_gather(down, "req", axis=1, axis_index_groups=planes)
        x_half = lax.all_gather(normed, "req", axis_index_groups=columns, tiled=True)
        x_all = lax.all_gather(x_half, "blk", axis=1, tiled=True)
    x_own = lax.dynamic_slice_in_dim(x_all, my_z * tok_rows, tok_rows, axis=0)

    logits = jnp.dot(x_all, router_full, preferred_element_type=f32)
    scores = jax.nn.sigmoid(logits)
    experts = jnp.arange(expert_count, dtype=jnp.int32)
    named = jnp.zeros(scores.shape, jnp.bool_)
    for k in range(routes.shape[1]):
        named = named | (routes_all[:, k : k + 1] == experts[None, :])
    chosen = jnp.where(named, scores, 0.0)
    gate_all = chosen / jnp.sum(chosen, axis=1, keepdims=True)
    gate_here = lax.dynamic_slice_in_dim(gate_all, my_z * plane, plane, axis=1)

    low_all = jnp.dot(x_own, adapter_full, preferred_element_type=f32)
    ends = jnp.cumsum(lengths[0])
    position = jnp.arange(tok_rows, dtype=jnp.int32)
    request = jnp.sum((position[:, None] >= ends[None, :]).astype(jnp.int32), axis=1)
    slots_req = jnp.arange(lengths.shape[1], dtype=jnp.int32)
    adapter_token = jnp.sum(
        jnp.where(request[:, None] == slots_req[None, :], adapter_ids[0][None, :], 0), axis=1
    )
    column_owner = jnp.arange(low_all.shape[1], dtype=jnp.int32) // RANK
    low = jnp.where(column_owner[None, :] == adapter_token[:, None], low_all, 0.0).astype(bf16)
    delta = jnp.dot(low, adapter_up, preferred_element_type=f32)

    shared_gate = jnp.dot(x_own, shared_gate_up[:, 0, :], preferred_element_type=f32)
    shared_up = jnp.dot(x_own, shared_gate_up[:, 1, :], preferred_element_type=f32)
    shared_hidden = (jax.nn.silu(shared_gate) * shared_up).astype(bf16)
    shared_terms = jnp.dot(shared_hidden, shared_down, preferred_element_type=f32)
    pieces = []
    for p in range(plane):
        gate_p = jnp.dot(x_all, gu_all[p, :, :half], preferred_element_type=f32)
        up_p = jnp.dot(x_all, gu_all[p, :, half:], preferred_element_type=f32)
        pieces.append((jax.nn.silu(gate_p) * up_p * gate_here[:, p : p + 1]).astype(bf16))
    hidden = jnp.concatenate(pieces, axis=1)
    terms = [
        jnp.dot(hidden, down_all[b].reshape(plane * half, feat_local), preferred_element_type=f32).astype(bf16)
        for b in range(2)
    ]
    shared_terms = shared_terms.astype(bf16)
    if plane == 4:
        parts = jnp.stack([x.reshape(DEPTH, tok_rows, feat_local) for x in terms])
        shared_parts = jnp.stack([shared_terms[:, :feat_local], shared_terms[:, feat_local:]])
        summed = give_back(parts, shared_parts)
    else:
        shared_out = lax.psum_scatter(shared_terms, "blk", scatter_dimension=1, tiled=True)
        terms = lax.psum_scatter(jnp.concatenate(terms, axis=1), "blk", scatter_dimension=1, tiled=True)
        summed = shared_out.astype(f32) + lax.psum_scatter(
            terms, "req", scatter_dimension=0, axis_index_groups=columns, tiled=True
        ).astype(f32)
    return (summed + 0.5 * delta).astype(bf16)


def solution(mesh):
    return jax.shard_map(
        body,
        mesh=mesh,
        in_specs=(
            P("req", "blk"),
            P("blk", None),
            P("blk", None),
            P(None, "blk"),
            P(None, None, "blk"),
            P("blk", None),
            P("req", "blk", None),
            P("req", None, "blk"),
            P("req", None),
            P("req", None),
            P("req", None),
        ),
        out_specs=P("req", "blk"),
        check_vma=False,
    )
```
